32 devices in a mesh: row: 8 (over y, x, core), col: 4 (over z).
Axes of the slice: x: 2, y: 2, z: 4, core: 2. Of those that a mesh axis runs over, the one named last changes fastest.
Arguments:
- slab: bfloat16 [2, 640, 640, 640], P(None, 'col', 'row'), may hold values from -6 to 6
- coef_virtual: bfloat16 [640, 576], replicated, may hold values from -0.25 to 0.25
- coef_occupied: bfloat16 [640, 64], replicated, may hold values from -0.25 to 0.25
- occ_level: int32 [64], replicated, may hold values from -160 to -16
- virt_level: int32 [576], replicated, may hold values from 16 to 192
- orbital_index: int32 [2], replicated, may hold values from 0 to 63
Outputs:
- back_slab: bfloat16 [2, 640, 640, 640], P(None, 'col', 'row')
The draws below stay inside these ranges and needn't reach their ends.
All inputs are finite; a program needn't handle non-finite values.
Results may differ from the reference program's by a relative error of at most 0.008.
Values may be sent and summed in bfloat16 or wider, within the bound.
A program may use at most 256 MiB of HBM per device.

```python
import jax
import jax.numpy as jnp

NB = 640
NO = 64
NV = 576
NI = 2


def place_ends(values, stream_key, least, largest):
    longest = values.shape.index(max(values.shape))
    spots = []
    for shift in (0, 1):
        where = [jax.random.randint(jax.random.fold_in(stream_key, axis), (), 0, length) for axis, length in enumerate(values.shape)]
        where[longest] = (where[longest] + shift) % values.shape[longest]
        spots.append(tuple(where))
    return values.at[spots[0]].set(least).at[spots[1]].set(largest)


def block_scale(key, shape, cuts, least, high):
    loudness = 1.0
    for dim, blocks in cuts:
        draws = jax.random.uniform(jax.random.fold_in(jax.random.fold_in(key, 6), dim), (blocks,), jnp.float32, least / len(cuts), high / len(cuts))
        loudness = loudness * jnp.repeat(jnp.exp(draws), shape[dim] // blocks).reshape((-1,) + (1,) * (len(shape) - 1 - dim))
    return loudness


def normal_values(own_key, dims, deviation, reach, cuts=(), kind=jnp.bfloat16):
    drawn = jax.random.normal(own_key, dims, jnp.float32) * deviation
    if len(cuts) > 0:
        drawn = block_scale(own_key, dims, cuts, -0.22, 0.18) * drawn
    return jnp.clip(drawn, min=-reach, max=reach).astype(kind)


def setup_inputs(seed: int = 0) -> dict:
    key_of = jax.random.split(jax.random.key(seed), 7)
    return {
        "slab": normal_values(key_of[0], (NI, NB, NB, NB), 1.0, 6.0, ((1, 4), (2, 8))),
        "coef_virtual": normal_values(key_of[1], (NB, NV), NB ** -0.5, 0.25),
        "coef_occupied": normal_values(key_of[2], (NB, NO), NB ** -0.5, 0.25),
        "occ_level": place_ends(jax.random.randint(key_of[3], (NO,), -160, -15), jax.random.fold_in(key_of[3], 1), -160, (-15) - 1).astype(jnp.int32),
        "virt_level": place_ends(jax.random.randint(key_of[4], (NV,), 16, 193), jax.random.fold_in(key_of[4], 1), 16, 192).astype(jnp.int32),
        "orbital_index": jax.random.randint(key_of[5], (NI,), 0, NO).astype(jnp.int32),
    }


def one_orbital(block, energy_i, coef_virtual, coef_occupied, eo, ev):
    first = jnp.dot(block.reshape(NB * NB, NB), coef_virtual, preferred_element_type=jnp.float32)
    first = first.astype(jnp.bfloat16).reshape(NB, NB * NV)
    second = jnp.dot(first.T, coef_occupied, preferred_element_type=jnp.float32).astype(jnp.bfloat16)
    third = jnp.dot(coef_virtual.T, second.reshape(NB, NV * NO), preferred_element_type=jnp.float32)
    third = third.reshape(NV, NV, NO)
    denom = ev[:, None, None] + ev[None, :, None] - energy_i - eo[None, None, :]
    amplitude = (third / denom).astype(jnp.bfloat16)
    back_one = jnp.dot(coef_virtual, amplitude.reshape(NV, NV * NO), preferred_element_type=jnp.float32)
    back_one = back_one.astype(jnp.bfloat16).reshape(NB * NV, NO)
    back_two = jnp.dot(back_one, coef_occupied.T, preferred_element_type=jnp.float32).astype(jnp.bfloat16)
    back_two = jnp.transpose(back_two.reshape(NB, NV, NB), (2, 0, 1)).reshape(NB * NB, NV)
    result = jnp.dot(back_two, coef_virtual.T, preferred_element_type=jnp.float32).astype(jnp.bfloat16)
    return result.reshape(NB, NB, NB)


def reference(slab, coef_virtual, coef_occupied, occ_level, virt_level, orbital_index):
    eo = occ_level.astype(jnp.float32) / 64.0
    ev = virt_level.astype(jnp.float32) / 64.0
    picks = orbital_index[:, None] == jnp.arange(NO, dtype=jnp.int32)[None, :]
    energy_i = jnp.sum(jnp.where(picks, eo[None, :], jnp.float32(0.0)), axis=1)
    outputs = []
    for orbit in range(NI):
        outputs.append(one_orbital(slab[orbit], energy_i[orbit], coef_virtual, coef_occupied, eo, ev))
    return jnp.stack(outputs, axis=0)
```

```python
import functools

import jax
import jax.numpy as jnp
from jax import lax
from jax.experimental import pallas as pl
from jax.experimental.pallas import tpu as pltpu
from jax.sharding import PartitionSpec as P

MESH = pl.DeviceIdType.MESH
LAG = 2


def greet(n_row, n_col, row, col):
    barrier = pltpu.get_barrier_semaphore()

    def hello(step, carry):
        other = lax.rem(row + step, n_row)
        pl.semaphore_signal(barrier, inc=1, device_id=(other, col), device_id_type=MESH)
        return carry

    lax.fori_loop(1, n_row, hello, 0)

    @pl.when(col > 0)
    def _():
        pl.semaphore_signal(barrier, inc=1, device_id=(row, col - 1), device_id_type=MESH)

    @pl.when(col < n_col - 1)
    def _():
        pl.semaphore_signal(barrier, inc=1, device_id=(row, col + 1), device_id_type=MESH)

    beside = jnp.where(col > 0, 1, 0) + jnp.where(col < n_col - 1, 1, 0)
    pl.semaphore_wait(barrier, n_row - 1 + beside)


def exchange(n_row, n_col, part, cv, cvt, ev_down, ev_across, shift, out, recv, whole, ready,
             in_line_send, in_line_recv, in_row_send, in_row_recv, in_own,
             out_line_send, out_line_recv, out_row_send, out_row_recv, out_own):
    row, col = lax.axis_index("row"), lax.axis_index("col")
    last = n_col - 1
    orbits, _, _, subs, width, basis_row, nb = part.shape
    per_orbit = n_row * subs
    chunks = orbits * per_orbit
    units = subs * width
    at_end = (col == 0) | (col == last)
    greet(n_row, n_col, row, col)

    def split(i):
        return i // per_orbit, lax.rem(i, per_orbit) // subs, lax.rem(i, subs)


    def in_target(i):
        return lax.rem(row + 1 + split(i)[1], n_row)

    def in_line(half, i, source):
        ahead = col + 1 if half == 0 else col - 1
        return pltpu.make_async_remote_copy(
            src_ref=source, dst_ref=recv.at[half, i],
            send_sem=in_line_send.at[half, i], recv_sem=in_line_recv.at[half, i],
            device_id=(row, ahead), device_id_type=MESH)

    def in_row(half, i):
        orbit, _, sub = split(i)
        return pltpu.make_async_remote_copy(
            src_ref=recv.at[half, i], dst_ref=whole.at[orbit, row, sub],
            send_sem=in_row_send.at[i], recv_sem=in_row_recv.at[orbit, row, sub],
            device_id=(in_target(i), col), device_id_type=MESH)

    def in_own_copy(half, i):
        orbit, _, sub = split(i)
        return pltpu.make_async_copy(
            recv.at[half, i], whole.at[orbit, row, sub], in_own.at[orbit, sub])

    def in_work(half, place, i):
        orbit, _, sub = split(i)
        target = in_target(i)

        @pl.when(place == 0)
        def _():
            in_line(half, i, part.at[orbit, half, target, sub]).start()

        @pl.when(place > 0)
        def _():
            in_line(half, i, recv.at[half, i]).wait_recv()
            mine = part[orbit, half, target, sub].astype(jnp.float32)
            recv[half, i] = (recv[half, i].astype(jnp.float32) + mine).astype(recv.dtype)

        @pl.when((place > 0) & (place < last))
        def _():
            in_line(half, i, recv.at[half, i]).start()

        @pl.when((place == last) & (target != row))
        def _():
            in_row(half, i).start()

        @pl.when((place == last) & (target == row))
        def _():
            in_own_copy(half, i).start()


    def arrived(orbit):
        def one(k, carry):
            source, sub = k // subs, lax.rem(k, subs)

            @pl.when(source != row)
            def _():
                pltpu.make_async_remote_copy(
                    src_ref=recv.at[0, 0], dst_ref=whole.at[orbit, source, sub],
                    send_sem=in_row_send.at[0], recv_sem=in_row_recv.at[orbit, source, sub],
                    device_id=(source, col), device_id_type=MESH).wait_recv()

            @pl.when(source == row)
            def _():
                pltpu.make_async_copy(
                    recv.at[0, 0], whole.at[orbit, source, sub], in_own.at[orbit, sub]).wait()
            return carry

        lax.fori_loop(0, per_orbit, one, 0)

    def dot(a, b):
        return jnp.dot(a, b, preferred_element_type=jnp.float32)

    def middle(orbit, k):
        sub, j = k // width, lax.rem(k, width)
        x = whole[orbit, :, sub, j]
        if basis_row % 16 == 0:
            x = x.reshape(n_row * basis_row, nb)
        else:
            x = x.astype(jnp.float32).reshape(n_row * basis_row, nb).astype(whole.dtype)
        second = dot(x, cv[...]).astype(whole.dtype)
        third = dot(cvt[...], second)
        denom = ev_down[...] + ev_across[...] - shift[orbit, k]
        amplitude = (third / denom).astype(whole.dtype)
        back_one = dot(cv[...], amplitude).astype(whole.dtype)
        back = dot(back_one, cvt[...]).reshape(n_row, basis_row, nb)
        ready[orbit, :, sub, j] = back.astype(ready.dtype)

    def middle_at(orbit, k):
        @pl.when(at_end & (k == 0))
        def _():
            arrived(orbit)

        @pl.when(at_end & (k >= 0) & (k < units))
        def _():
            middle(orbit, k)


    def out_source(i):
        return lax.rem(row - split(i)[1] + n_row, n_row)

    def out_target(i):
        return lax.rem(row + split(i)[1], n_row)

    def out_line(half, i):
        ahead = col - 1 if half == 0 else col + 1
        orbit, _, sub = split(i)
        block = out.at[orbit, half, out_source(i), sub]
        return pltpu.make_async_remote_copy(
            src_ref=block, dst_ref=block,
            send_sem=out_line_send.at[half, i], recv_sem=out_line_recv.at[half, i],
            device_id=(row, ahead), device_id_type=MESH)

    def out_row(half, i):
        orbit, _, sub = split(i)
        target = out_target(i)
        return pltpu.make_async_remote_copy(
            src_ref=ready.at[orbit, target, sub], dst_ref=out.at[orbit, half, row, sub],
            send_sem=out_row_send.at[i], recv_sem=out_row_recv.at[i],
            device_id=(target, col), device_id_type=MESH)

    def out_own_copy(half, i):
        orbit, _, sub = split(i)
        return pltpu.make_async_copy(
            ready.at[orbit, row, sub], out.at[orbit, half, row, sub], out_own.at[orbit, sub])

    def give(half, i):
        @pl.when(split(i)[1] == 0)
        def _():
            out_own_copy(half, i).start()

        @pl.when(split(i)[1] != 0)
        def _():
            out_row(half, i).start()

    def take(half, i):
        orbit, _, sub = split(i)

        @pl.when(split(i)[1] == 0)
        def _():
            out_own_copy(half, i).wait()

        @pl.when(split(i)[1] != 0)
        def _():
            pltpu.make_async_remote_copy(
                src_ref=ready.at[orbit, row, sub], dst_ref=out.at[orbit, half, out_source(i), sub],
                send_sem=out_row_send.at[i], recv_sem=out_row_recv.at[i],
                device_id=(out_source(i), col), device_id_type=MESH).wait_recv()


    def in_step(s, carry):
        for half in (0, 1):
            place = col if half == 0 else last - col
            i = s - LAG * place

            @pl.when((i >= 0) & (i < chunks))
            def _():
                in_work(half, place, i)
        for orbit in range(orbits - 1):
            middle_at(orbit, s - ((orbit + 1) * per_orbit + LAG * last + 2))
        return carry

    lax.fori_loop(0, chunks + LAG * last, in_step, 0)

    first = max(1, min(6, per_orbit - units - 1))

    def open_(i, carry):
        for half in (0, 1):
            place = last - col if half == 0 else col

            @pl.when(place == 0)
            def _():
                give(half, i)
        return carry

    lax.fori_loop(0, first, open_, 0)

    def out_step(s, carry):
        for half in (0, 1):
            place = last - col if half == 0 else col
            i = s - LAG * place

            @pl.when((place == 0) & (i + first < chunks))
            def _():
                give(half, i + first)

            @pl.when((place == 0) & (i < chunks))
            def _():
                take(half, i)

            @pl.when((place > 0) & (i >= 0) & (i < chunks))
            def _():
                out_line(half, i).wait_recv()

            @pl.when((place < last) & (i >= 0) & (i < chunks))
            def _():
                out_line(half, i).start()
        middle_at(orbits - 1, s - 1)
        return carry

    lax.fori_loop(0, chunks + LAG * last, out_step, 0)

    def drain(i, carry):
        for half in (0, 1):
            place = col if half == 0 else last - col

            @pl.when(place < last)
            def _():
                in_line(half, i, recv.at[half, i]).wait_send()

            @pl.when((place == last) & (in_target(i) != row))
            def _():
                in_row(half, i).wait_send()

            @pl.when(place > 0)
            def _():
                out_line(half, i).wait_send()

            @pl.when((place == last) & (split(i)[1] != 0))
            def _():
                out_row(half, i).wait_send()
        return carry

    lax.fori_loop(0, chunks, drain, 0)


def run_exchange(n_row, n_col, part, cv, ev, shift):
    orbits, _, _, subs = part.shape[:4]
    block = part.shape[4:]
    chunks = orbits * n_row * subs
    dma = pltpu.SemaphoreType.DMA
    vmem = pl.BlockSpec(memory_space=pltpu.VMEM)
    held = (orbits, n_row, subs) + block
    return pl.pallas_call(
        functools.partial(exchange, n_row, n_col),
        out_shape=jax.ShapeDtypeStruct(part.shape, part.dtype),
        in_specs=[vmem] * 5 + [pl.BlockSpec(memory_space=pltpu.SMEM)],
        out_specs=pl.BlockSpec(memory_space=pl.ANY),
        scratch_shapes=[
            pltpu.VMEM((2, chunks) + block, part.dtype),
            pltpu.VMEM(held, part.dtype), pltpu.VMEM(held, part.dtype),
            dma((2, chunks)), dma((2, chunks)), dma((chunks,)), dma((orbits, n_row, subs)), dma((orbits, subs)),
            dma((2, chunks)), dma((2, chunks)), dma((chunks,)), dma((chunks,)), dma((orbits, subs)),
        ],
        compiler_params=pltpu.CompilerParams(
            collective_id=0, has_side_effects=True, vmem_limit_bytes=58 * 1024 * 1024),
        name="exchange",
    )(part, cv, cv.T, ev[:, None], ev[None, :], shift)


def local(slab, coef_virtual, coef_occupied, occ_level, virt_level, orbital_index):
    n_row = lax.axis_size("row")
    n_col = lax.axis_size("col")
    orbits, basis_col, basis_row, nb = slab.shape
    no = coef_occupied.shape[1]
    eo = occ_level.astype(jnp.float32) / 64.0
    ev = virt_level.astype(jnp.float32) / 64.0
    picks = orbital_index[:, None] == jnp.arange(no, dtype=jnp.int32)[None, :]
    energy_i = jnp.sum(jnp.where(picks, eo[None, :], jnp.float32(0.0)), axis=1)
    col = lax.axis_index("col")
    row = lax.axis_index("row")
    occ_mine = lax.dynamic_slice_in_dim(coef_occupied, col * basis_col, basis_col, 0)
    j_mine = no // (2 * n_row)
    subs = 2 if j_mine % 2 == 0 else 1
    j_start = jnp.where(col == 0, no // 2, 0) + row * j_mine
    eo_mine = lax.dynamic_slice_in_dim(eo, j_start, j_mine, 0)

    part = jnp.einsum(
        "lj,olmn->ojmn", occ_mine, slab, preferred_element_type=jnp.float32
    ).astype(jnp.bfloat16)
    part = part.reshape(orbits, 2, n_row, subs, j_mine // subs, basis_row, nb)
    shift = energy_i[:, None] + eo_mine[None, :]
    back = run_exchange(n_row, n_col, part, coef_virtual, ev, shift)
    back = back.reshape(orbits, no, basis_row, nb)
    return jnp.einsum(
        "lj,ojmn->olmn", occ_mine, back, preferred_element_type=jnp.float32
    ).astype(jnp.bfloat16)


def solution(mesh):
    placed = (P(None, "col", "row", None), P(), P(), P(), P(), P())
    return jax.shard_map(
        local, mesh=mesh, in_specs=placed, out_specs=P(None, "col", "row", None), check_vma=False
    )
```
